256 devices in a mesh: group: 4 (over y), section: 2 (over z_lo), tp: 32 (over z_hi, x, core).
Axes of the slice: x: 4, y: 4, z: 8 (z_hi: 4, z_lo: 2; z = z_hi * 2 + z_lo), core: 2. Of those that a mesh axis runs over, the one named last changes fastest.
Arguments:
- inputs: bfloat16 [1024, 6144], P(('group', 'tp')), may hold values from -6 to 6
- lengths: int32 [4], P('group'), may hold values from 1 to 256
- norm_gain: float32 [2, 6144], P('section'), may hold values from 0.1 to 1.9
- base_weight: bfloat16 [2, 2, 6144, 14336], P('section', None, None, 'tp'), may hold values from -0.078125 to 0.078125
- factor_p: bfloat16 [2, 2, 64, 6144], P('section', None, 'group', 'tp'), may hold values from -0.119628906 to 0.119628906
- factor_q: bfloat16 [2, 2, 64, 14336], P('section', None, 'group', 'tp'), may hold values from -0.119628906 to 0.119628906
Outputs:
- mixed: bfloat16 [2, 1024, 6144], P('section', ('group', 'tp'))
The draws below stay inside these ranges and needn't reach their ends.
All inputs are finite; a program needn't handle non-finite values.
Results may differ from the reference program's by a relative error of at most 0.024.
Values may be sent and summed in bfloat16 or wider, within the bound.
A program may use at most 128 MiB of HBM per device.

```python
import jax
import jax.numpy as jnp
from jax import lax

D = 6144
FFW = 14336
R = 64
SEQS = 1
LEN = 256
TOKENS = 1024
N_GROUP = 4
N_TP = 32


def plant(result, rng, low, high):
    index_at = [jax.random.randint(jax.random.fold_in(rng, axis), (), 0, length) for axis, length in enumerate(result.shape)]
    longest = result.shape.index(max(result.shape))
    beside = index_at[:longest] + [(index_at[longest] + 1) % result.shape[longest]] + index_at[longest + 1:]
    return result.at[tuple(index_at)].set(low).at[tuple(beside)].set(high)


def steps_of(rng, extent, split, low, top_value):
    factor_of, own = 1.0, jax.random.fold_in(rng, 6)
    for position, shards_of in split:
        heights = jnp.exp(jax.random.uniform(jax.random.fold_in(own, position), (shards_of,), jnp.float32, low / len(split), top_value / len(split)))
        factor_of = factor_of * jnp.repeat(heights, extent[position] // shards_of).reshape([-1 if axis == position else 1 for axis in range(len(extent))])
    return factor_of


def normal_values(key, shape, spread, reach, shards=(), kind=jnp.bfloat16):
    values = spread * jax.random.normal(key, shape, jnp.float32)
    if shards:
        values = values * steps_of(key, shape, shards, -0.22, 0.18)
    return jnp.clip(values, -reach, reach).astype(kind)


def setup_inputs(seed: int = 0) -> dict:
    seeds = jax.random.split(jax.random.key(seed), 7)
    return {
        "inputs": normal_values(seeds[0], (TOKENS, D), 1.0, 6.0, ((0, 128),)),
        "lengths": plant(jax.random.randint(seeds[1], (N_GROUP * SEQS,), 1, LEN + 1), jax.random.fold_in(seeds[1], 1), 1, LEN).astype(jnp.int32),
        "norm_gain": jnp.clip(1.0 + 0.18 * jax.random.normal(seeds[2], (2, D), jnp.float32), 0.1, 1.9),
        "base_weight": normal_values(seeds[3], (2, 2, D, FFW), D ** -0.5, 0.078125, ((0, 2), (3, 32))),
        "factor_p": normal_values(seeds[4], (2, 2, R, D), ((0.25 / (R * D) ** 0.5) ** 0.5), 0.119628906, ((0, 2), (2, 4), (3, 32))),
        "factor_q": normal_values(seeds[5], (2, 2, R, FFW), ((0.25 / (R * D) ** 0.5) ** 0.5), 0.119628906, ((0, 2), (2, 4), (3, 32))),
    }


adapter_scale = 2.0
norm_eps = 1e-05

def merge_weight(frozen_matrix, left, right):
    adapter_update = lax.dot_general(left, right, (((0,), (0,)), ((), ())), preferred_element_type=jnp.float32)
    return (frozen_matrix.astype(jnp.float32) + adapter_scale * adapter_update).astype(jnp.bfloat16)

def apply_layer(state, gain, merged_up, merged_down, valid):
    resid = state.astype(jnp.float32)
    mean_square = lax.optimization_barrier(jnp.mean(resid * resid, axis=-1, keepdims=True))
    normed = (resid * lax.rsqrt(mean_square + norm_eps) * gain).astype(jnp.bfloat16)
    before = jnp.dot(normed, merged_up, preferred_element_type=jnp.float32)
    hidden = (jax.nn.silu(before) * valid[:, None]).astype(jnp.bfloat16)
    width_per_block = FFW // N_TP
    summed = jnp.zeros((state.shape[0], D), jnp.float32)
    for block_index in range(N_TP):
        hidden_block = hidden[:, block_index * width_per_block:(block_index + 1) * width_per_block]
        weight_block = merged_down[:, block_index * width_per_block:(block_index + 1) * width_per_block]
        partial_product = lax.dot_general(hidden_block, weight_block, (((1,), (1,)), ((), ())), preferred_element_type=jnp.float32)
        rounded = lax.optimization_barrier(partial_product.astype(jnp.bfloat16))
        summed = summed + rounded.astype(jnp.float32)
    return (resid + summed).astype(jnp.bfloat16)

def reference(inputs, lengths, norm_gain, base_weight, factor_p, factor_q):
    row_count = inputs.shape[0]
    token_position = jnp.arange(row_count, dtype=jnp.int32) % LEN
    valid = (token_position < jnp.repeat(lengths, LEN)).astype(jnp.float32)
    state = inputs
    layer_outputs = []
    for layer_index in range(2):
        merged_up = merge_weight(base_weight[layer_index, 0], factor_p[layer_index, 0], factor_q[layer_index, 0])
        merged_down = merge_weight(base_weight[layer_index, 1], factor_p[layer_index, 1], factor_q[layer_index, 1])
        state = apply_layer(state, norm_gain[layer_index], merged_up, merged_down, valid)
        layer_outputs.append(state)
    return jnp.stack(layer_outputs)
```

```python
import functools

import jax
import jax.numpy as jnp
from jax import lax
from jax.experimental import pallas as pl
from jax.experimental.pallas import tpu as pltpu
from jax.sharding import PartitionSpec as P

adapter_scale = 2.0
norm_eps = 1e-05
NX = 4

BF, F32 = jnp.bfloat16, jnp.float32
NT = (((1,), (1,)), ((), ()))


def kernel(
    nz, nx, ng,
    x_ref, len_ref, gain_ref, w_ref, p_ref, q_ref,
    out_ref,
    st, nrm, tn, xg, wu, wd, ppad, pg, qg,
    acc, hid, usc, tsend, trecv, spart, r1, s1, r2, fs, fr, res, rsend, rrecv,
    wsem, tw_s, tw_r, ag_s, ag_r, fw_s, fw_r, pt_s, pt_r, px_s, px_r, qy_s, qy_r,
    rt_s, rt_r, rs_s, rs_r, fin_s, fin_r, rel_s, rel_r,
):
    g = lax.axis_index("group")
    sec = lax.axis_index("section")
    t = lax.axis_index("tp")
    c = lax.rem(t, 2)
    chip = lax.div(t, 2)
    xi = lax.rem(chip, nx)
    zi = lax.div(chip, nx)
    o = 1 - c
    d_model = x_ref.shape[1]
    qc = d_model // 4
    hc = d_model // 2
    rows = nz * nx * 16
    pc = d_model // (nz * nx)
    chunks = qc // pc

    def tp_of(z, x, core):
        return (z * nx + x) * 2 + core

    twin = {"tp": tp_of(zi, xi, o)}

    def xpeer(d):
        return lax.rem(xi + d, nx)

    def zpeer(d):
        return lax.rem(zi + d, nz)

    def ypeer(d):
        return lax.rem(g + d, ng)

    def to_x(d):
        return {"tp": tp_of(zi, xpeer(d), c)}

    def to_z(d):
        return {"tp": tp_of(zpeer(d), xi, c)}

    def to_y(d):
        return {"group": ypeer(d)}

    sends = []

    def rcopy(src, dst, ss, rs, dev):
        return pltpu.make_async_remote_copy(
            src_ref=src, dst_ref=dst, send_sem=ss, recv_sem=rs,
            device_id=dev, device_id_type=pl.DeviceIdType.MESH,
        )

    def go(copy):
        copy.start()
        sends.append(copy)
        return copy

    cu = pltpu.make_async_copy(w_ref.at[0, 0], wu, wsem.at[0])
    cd = pltpu.make_async_copy(w_ref.at[0, 1], wd, wsem.at[1])
    cu.start()
    cd.start()

    barrier = pltpu.get_barrier_semaphore()
    peers = [twin]
    peers += [to_x(d) for d in range(1, nx)]
    peers += [to_z(d) for d in range(1, nz)]
    peers += [to_y(d) for d in range(1, ng)]
    peers += [{"section": 1 - sec}]
    for dev in peers:
        pl.semaphore_signal(barrier, inc=1, device_id=dev, device_id_type=pl.DeviceIdType.MESH)
    pl.semaphore_wait(barrier, len(peers))

    qsends = [go(rcopy(q_ref, qg.at[:, g], qy_s.at[d - 1], qy_r.at[d - 1], to_y(d))) for d in range(1, ng)]
    qg[:, g] = q_ref[...]

    ptw = go(rcopy(p_ref, ppad, pt_s.at[0], pt_r.at[0], twin))

    def p_own():
        ptw.wait_recv()
        mine = (p_ref[...].astype(F32) + ppad[...].astype(F32)).astype(BF)
        pg[:, g, zi, xi] = mine

    pxs = [rcopy(pg.at[c, g, zi, xi], pg.at[c, g, zi, xi], px_s.at[0, d - 1], px_r.at[0, d - 1], to_x(d)) for d in range(1, nx)]
    pzs = [rcopy(pg.at[c, g, zi], pg.at[c, g, zi], px_s.at[1, d - 1], px_r.at[1, d - 1], to_z(d)) for d in range(1, nz)]
    pys = [rcopy(pg.at[c, g], pg.at[c, g], px_s.at[2, d - 1], px_r.at[2, d - 1], to_y(d)) for d in range(1, ng)]
    ptf = [rcopy(pg.at[c, lax.rem(g + d, ng)], pg.at[c, lax.rem(g + d, ng)], pt_s.at[1 + d], pt_r.at[1 + d], twin) for d in range(1, ng)]
    ptx = [
        rcopy(pg.at[c, g, zi, xpeer(d)], pg.at[c, g, zi, xpeer(d)], px_s.at[3, d - 1], px_r.at[3, d - 1], twin) for d in range(1, nx)
    ]
    ptz = [
        rcopy(pg.at[c, g, zpeer(d)], pg.at[c, g, zpeer(d)], px_s.at[4, d - 1], px_r.at[4, d - 1], twin) for d in range(1, nz)
    ]

    def start(copies):
        for k in copies:
            k.start()

    def p_x():
        start(pxs)

    def p_z():
        for k, f in zip(pxs, ptx):
            k.wait_recv()
        start(pzs)
        start(ptx)

    def p_y():
        for k in pzs:
            k.wait_recv()
        start(pys)
        start(ptz)

    def p_t():
        for k in pys:
            k.wait_recv()
        start(ptf)

    sends.extend(pxs + pzs + pys + ptf + ptx + ptz)

    p_own()
    p_x()

    relay = rcopy(rsend, rrecv, rel_s.at[0], rel_r.at[0], {"section": 1})

    @pl.when(sec == 0)
    def _():
        st[...] = x_ref[...].astype(F32)

    @pl.when(sec == 1)
    def _():
        p_z()
        p_y()
        p_t()
        relay.wait_recv()
        both = rrecv[...].astype(F32)
        st[:, :hc] = both[:8]
        st[:, hc:] = both[8:]

    resid = st[...]
    mean_square = jnp.mean(resid * resid, axis=-1, keepdims=True)
    nrm[...] = resid * lax.rsqrt(mean_square + norm_eps) * gain_ref[...]
    tw = go(rcopy(nrm, tn, tw_s.at[0], tw_r.at[0], twin))

    @pl.when(sec == 0)
    def _():
        p_z()

    tw.wait_recv()
    for q in range(4):
        cols = slice(q * qc, (q + 1) * qc)
        mine, theirs = nrm[:, cols], tn[:, cols]
        top = jnp.where(c == 0, mine, theirs)
        bottom = jnp.where(c == 0, theirs, mine)
        xg[q, zi, xi] = jnp.concatenate([top, bottom], axis=0).astype(BF)

    qa, qb = 2 * c, 2 * c + 1
    a1 = [go(rcopy(xg.at[qa, zi, xi], xg.at[qa, zi, xi], ag_s.at[0, d - 1], ag_r.at[0, d - 1], to_x(d))) for d in range(1, nx)]
    b1 = [go(rcopy(xg.at[qb, zi, xi], xg.at[qb, zi, xi], ag_s.at[1, d - 1], ag_r.at[1, d - 1], to_z(d))) for d in range(1, nz)]

    def forward(ref, i, d):
        return go(rcopy(ref, ref, fw_s.at[i, d - 1], fw_r.at[i, d - 1], twin))

    fwd = []
    for k in a1:
        k.wait_recv()
    a2 = [go(rcopy(xg.at[qa, zi], xg.at[qa, zi], ag_s.at[2, d - 1], ag_r.at[2, d - 1], to_z(d))) for d in range(1, nz)]
    for k in b1:
        k.wait_recv()
    b2 = [go(rcopy(xg.at[qb, :, xi], xg.at[qb, :, xi], ag_s.at[3, d - 1], ag_r.at[3, d - 1], to_x(d))) for d in range(1, nx)]
    for d in range(1, nx):
        fwd.append(forward(xg.at[qa, zi, lax.rem(xi + nx - d, nx)], 0, d))
    for d in range(1, nz):
        fwd.append(forward(xg.at[qb, lax.rem(zi + nz - d, nz), xi], 1, d))

    @pl.when(sec == 0)
    def _():
        p_y()

    for d in range(1, nz):
        a2[d - 1].wait_recv()
        fwd.append(forward(xg.at[qa, lax.rem(zi + nz - d, nz)], 2, d))
    for d in range(1, nx):
        b2[d - 1].wait_recv()
        fwd.append(forward(xg.at[qb, :, lax.rem(xi + nx - d, nx)], 3, d))

    cu.wait()

    def up(q):
        lhs = xg[q].reshape(rows, qc)
        return jnp.dot(lhs, wu[pl.ds(pl.multiple_of(q * qc, 128), qc), :], preferred_element_type=F32)

    acc[...] = up(qa)
    acc[...] += up(qb)

    @pl.when(sec == 0)
    def _():
        p_t()

    for k in fwd:
        k.wait_recv()
    acc[...] += up(2 * o)
    acc[...] += up(2 * o + 1)
    for k in qsends + ptf + ptx + ptz:
        k.wait_recv()

    def low(i, s):
        q = lax.div(i, chunks)
        j = lax.rem(i, chunks)
        lhs = xg[q, :, :, :, pl.ds(pl.multiple_of(j * pc, 128), pc)].reshape(rows, pc)
        z, x = lax.div(i, nx), lax.rem(i, nx)
        rhs = pg[0, :, z, x].reshape(ng * 16, pc)
        return s + lax.dot_general(lhs, rhs, NT, preferred_element_type=F32)

    s = lax.fori_loop(0, nz * nx, low, jnp.zeros((rows, ng * 16), F32))
    s_hi = s.astype(BF)
    s_lo = (s - s_hi.astype(F32)).astype(BF)
    q_up = qg[0].reshape(ng * 16, qg.shape[3])
    q_down = qg[1].reshape(ng * 16, qg.shape[3])
    low_rank = jnp.dot(s_hi, q_up, preferred_element_type=F32) + jnp.dot(s_lo, q_up, preferred_element_type=F32)
    before = acc[...] + adapter_scale * low_rank
    valid = (lax.broadcasted_iota(jnp.int32, (rows, 1), 0) < len_ref[0]).astype(F32)
    hidden = (before / (1.0 + jnp.exp(-before)) * valid).astype(BF)
    hid[...] = hidden
    usc[...] = (adapter_scale * lax.dot_general(hidden, q_down, NT, preferred_element_type=F32)).astype(BF)
    cd.wait()

    def down(i):
        at = pl.multiple_of(i * pc, 128)
        main = lax.dot_general(hid[...], wd[pl.ds(at, pc), :], NT, preferred_element_type=F32)
        z, x = lax.div(i, nx), lax.rem(i, nx)
        return main + jnp.dot(usc[...], pg[1, :, z, x].reshape(ng * 16, pc), preferred_element_type=F32)

    sent = []
    for h in range(2):
        def twin_part(j, carry, h=h):
            i = (2 * o + h) * chunks + j
            tsend[h, :, :, :, pl.ds(pl.multiple_of(j * pc, 128), pc)] = down(i).astype(BF).reshape(nz, nx, 16, pc)
            return carry

        lax.fori_loop(0, chunks, twin_part, 0)
        sent.append(go(rcopy(tsend.at[h], trecv.at[h], rt_s.at[h], rt_r.at[h], twin)))

    p1 = [[], []]
    for h in range(2):
        sent[h].wait_recv()

        def own_part(j, carry, h=h):
            i = (2 * c + h) * chunks + j
            at = pl.ds(pl.multiple_of(j * pc, 128), pc)
            both = down(i).astype(BF).astype(F32).reshape(nz, nx, 16, pc) + trecv[h, :, :, :, at].astype(F32)
            spart[h, :, :, :, at] = both.astype(BF)
            return carry

        lax.fori_loop(0, chunks, own_part, 0)
        if h == 0:
            for d in range(1, nz):
                p1[0].append(go(rcopy(spart.at[0, zpeer(d)], r1.at[0, d - 1], rs_s.at[0, d - 1], rs_r.at[0, d - 1], to_z(d))))
        else:
            for d in range(1, nx):
                p1[1].append(go(rcopy(spart.at[1, :, xpeer(d)], r1.at[1, d - 1], rs_s.at[1, d - 1], rs_r.at[1, d - 1], to_x(d))))

    p2 = [[], []]
    for h in range(2):
        for k in p1[h]:
            k.wait_recv()
        total = spart[0, zi].astype(F32) if h == 0 else spart[1, :, xi].astype(F32)
        for k in range(len(p1[h])):
            total = total + r1[h, k].astype(F32)
        s1[h] = total.astype(BF)
        if h == 0:
            for d in range(1, nx):
                p2[0].append(go(rcopy(s1.at[0, xpeer(d)], r2.at[0, d - 1], rs_s.at[2, d - 1], rs_r.at[2, d - 1], to_x(d))))
        else:
            for d in range(1, nz):
                p2[1].append(go(rcopy(s1.at[1, zpeer(d)], r2.at[1, d - 1], rs_s.at[3, d - 1], rs_r.at[3, d - 1], to_z(d))))

    for h in range(2):
        for k in p2[h]:
            k.wait_recv()
        total = s1[h, xi if h == 0 else zi].astype(F32)
        for k in range(len(p2[h])):
            total = total + r2[h, k].astype(F32)
        fs[0, :, h * qc:(h + 1) * qc] = total[:8]
        fs[1, :, h * qc:(h + 1) * qc] = total[8:]

    fin = go(rcopy(fs.at[o], fr, fin_s.at[0], fin_r.at[0], twin))
    mine_at = pl.ds(pl.multiple_of(c * hc, 128), hc)
    other_at = pl.ds(pl.multiple_of(o * hc, 128), hc)
    res[:, mine_at] = st[:, mine_at] + fs[c]
    fin.wait_recv()
    res[:, other_at] = st[:, other_at] + fr[...]
    out_ref[0] = res[...].astype(BF)

    @pl.when(sec == 0)
    def _():
        rsend[...] = jnp.concatenate([res[:, :hc], res[:, hc:]], axis=0).astype(BF)
        relay.start()
        relay.wait_send()

    for k in sends:
        k.wait_send()


def body(inputs, lengths, norm_gain, base_weight, factor_p, factor_q):
    ng = lax.axis_size("group")
    nx = NX
    nz = lax.axis_size("tp") // 2 // nx
    d_model = inputs.shape[1]
    ffw = base_weight.shape[3]
    rows = nz * nx * 16
    assert nx == nz
    qc, hc, pc = d_model // 4, d_model // 2, d_model // (nz * nx)
    core = lax.rem(lax.axis_index("tp"), 2)
    p = factor_p[0]
    blank = jnp.zeros_like(p)
    p_padded = jnp.where(
        core == 0, jnp.concatenate([p, blank], axis=2), jnp.concatenate([blank, p], axis=2)
    )
    vmem = pl.BlockSpec(memory_space=pltpu.VMEM)
    dma = pltpu.SemaphoreType.DMA
    n3 = max(nx, nz, ng) - 1
    out = pl.pallas_call(
        functools.partial(kernel, nz, nx, ng),
        out_shape=jax.ShapeDtypeStruct((1, 8, d_model), BF),
        in_specs=[
            vmem,
            pl.BlockSpec(memory_space=pltpu.SMEM),
            vmem,
            pl.BlockSpec(memory_space=pl.ANY),
            vmem,
            vmem,
        ],
        out_specs=vmem,
        scratch_shapes=[
            pltpu.VMEM((8, d_model), F32),
            pltpu.VMEM((8, d_model), F32),
            pltpu.VMEM((8, d_model), F32),
            pltpu.VMEM((4, nz, nx, 16, qc), BF),
            pltpu.VMEM((d_model, ffw), BF),
            pltpu.VMEM((d_model, ffw), BF),
            pltpu.VMEM((2, 16, pc), BF),
            pltpu.VMEM((2, ng, nz, nx, 16, pc), BF),
            pltpu.VMEM((2, ng, 16, ffw), BF),
            pltpu.VMEM((rows, ffw), F32),
            pltpu.VMEM((rows, ffw), BF),
            pltpu.VMEM((rows, ng * 16), BF),
            pltpu.VMEM((2, nz, nx, 16, qc), BF),
            pltpu.VMEM((2, nz, nx, 16, qc), BF),
            pltpu.VMEM((2, nz, nx, 16, qc), BF),
            pltpu.VMEM((2, n3, nx, 16, qc), BF),
            pltpu.VMEM((2, nx, 16, qc), BF),
            pltpu.VMEM((2, n3, 16, qc), BF),
            pltpu.VMEM((2, 8, hc), F32),
            pltpu.VMEM((8, hc), F32),
            pltpu.VMEM((8, d_model), F32),
            pltpu.VMEM((16, hc), BF),
            pltpu.VMEM((16, hc), BF),
            dma((2,)),
            dma((1,)), dma((1,)),
            dma((4, n3)), dma((4, n3)),
            dma((4, n3)), dma((4, n3)),
            dma((6,)), dma((6,)),
            dma((5, n3)), dma((5, n3)),
            dma((n3,)), dma((n3,)),
            dma((2,)), dma((2,)),
            dma((4, n3)), dma((4, n3)),
            dma((1,)), dma((1,)),
            dma((1,)), dma((1,)),
        ],
        compiler_params=pltpu.CompilerParams(
            collective_id=0, has_side_effects=True, vmem_limit_bytes=56 * 1024 * 1024
        ),
    )(inputs, lengths, norm_gain, base_weight, p_padded, factor_q[0])
    return out


def solution(mesh):
    return jax.shard_map(
        body,
        mesh=mesh,
        in_specs=(
            P(("group", "tp"), None),
            P("group"),
            P("section", None),
            P("section", None, None, "tp"),
            P("section", None, "group", "tp"),
            P("section", None, "group", "tp"),
        ),
        out_specs=P("section", ("group", "tp"), None),
        check_vma=False,
    )
```

```python
import functools

import jax
import jax.numpy as jnp
from jax import lax
from jax.experimental import pallas as pl
from jax.experimental.pallas import tpu as pltpu
from jax.sharding import PartitionSpec as P

adapter_scale = 2.0
norm_eps = 1e-05
NX = 4

BF, F32 = jnp.bfloat16, jnp.float32
NT = (((1,), (1,)), ((), ()))
STREAMS, A = 3, 1
ORDER = (0, 1, 2)
NEAR_FIRST = (1, 3, 2)


def kernel(
    nz, nx, ng,
    x_ref, len_ref, gain_ref, w_ref, p_ref, q_ref,
    out_ref,
    xs, xt, xg, wp, psend, precv, qg, acc, hid, tsend, trecv, spart, r1, s1, r2, fb, fs, fr,
    wsem, bar_s, bar_r, g1_s, g1_r, g2_s, g2_r, f1_s, f1_r, f2_s, f2_r,
    pp_s, pp_r, pt_s, pt_r, qy_s, qy_r, rt_s, rt_r, e1_s, e1_r, e2_s, e2_r, rel_s,
):
    g = lax.axis_index("group")
    sec = lax.axis_index("section")
    t = lax.axis_index("tp")
    c = lax.rem(t, 2)
    o = 1 - c
    chip = lax.div(t, 2)
    xi = lax.rem(chip, nx)
    zi = lax.div(chip, nx)
    d_model = x_ref.shape[1]
    ffw = w_ref.shape[1]
    hc = d_model // 2
    sc = hc // STREAMS
    rows = nz * nx * 16
    pc = d_model // (nz * nx)

    def tp_of(z, x, core):
        return (z * nx + x) * 2 + core

    def xpeer(d):
        return lax.rem(xi + d, nx)

    def zpeer(d):
        return lax.rem(zi + d, nz)

    def xfrom(d):
        return lax.rem(xi + nx - d, nx)

    def zfrom(d):
        return lax.rem(zi + nz - d, nz)

    twin = {"tp": tp_of(zi, xi, o)}

    def to_x(d):
        return {"tp": tp_of(zi, xpeer(d), c)}

    def to_z(d):
        return {"tp": tp_of(zpeer(d), xi, c)}

    def to_y(d):
        return {"group": lax.rem(g + d, ng)}

    def rcopy(src, dst, ss, rs, dev):
        return pltpu.make_async_remote_copy(
            src_ref=src, dst_ref=dst, send_sem=ss, recv_sem=rs,
            device_id=dev, device_id_type=pl.DeviceIdType.MESH,
        )

    sends = []

    def go(copy):
        copy.start()
        sends.append(copy)
        return copy

    cw = [pltpu.make_async_copy(w_ref.at[k], wp.at[k, 0:ffw], wsem.at[k]) for k in range(2)]
    cw[0].start()
    cw[1].start()

    barrier = pltpu.get_barrier_semaphore()
    peers = [twin]
    peers += [to_x(d) for d in range(1, nx)]
    peers += [to_z(d) for d in range(1, nz)]
    peers += [to_y(d) for d in range(1, ng)]
    peers += [{"section": 1 - sec}]
    peers += [{"section": 1 - sec, **to_x(d)} for d in range(1, nx)]
    peers += [{"section": 1 - sec, **to_z(d)} for d in range(1, nz)]
    for dev in peers:
        pl.semaphore_signal(barrier, inc=1, device_id=dev, device_id_type=pl.DeviceIdType.MESH)

    pf = p_ref[...].astype(F32)
    blank = jnp.zeros_like(pf)
    psend[...] = jnp.where(
        c == 0, jnp.concatenate([pf, blank], axis=2), jnp.concatenate([blank, pf], axis=2)
    ).astype(BF)
    mine_at = pl.ds(pl.multiple_of(c * hc, 128), hc)
    other_at = pl.ds(pl.multiple_of(o * hc, 128), hc)
    xs[...] = x_ref[:, other_at].astype(F32)
    qg[:, g] = q_ref[...]

    pl.semaphore_wait(barrier, len(peers))

    xtw = rcopy(xs, xt, bar_s.at[0], bar_r.at[0], twin)

    @pl.when(sec == 0)
    def _():
        xtw.start()

    ptw = go(rcopy(psend, precv, bar_s.at[1], bar_r.at[1], twin))
    qsends = [go(rcopy(q_ref, qg.at[:, g], qy_s.at[d - 1], qy_r.at[d - 1], to_y(d))) for d in range(1, ng)]

    def own(s):
        return xg.at[c, s, zi, xi]

    g1 = [
        [rcopy(own(s), own(s), g1_s.at[s, d], g1_r.at[s, d], to_x(d) if s == A else to_z(d)) for d in range(nx)]
        for s in range(STREAMS)
    ]

    @pl.when(sec == 0)
    def _():
        xtw.wait_recv()
        for s in range(STREAMS):
            mine = x_ref[:, pl.ds(pl.multiple_of(c * hc + s * sc, 128), sc)].astype(F32)
            theirs = xt[:, s * sc:(s + 1) * sc]
            top = jnp.where(c == 0, mine, theirs)
            bottom = jnp.where(c == 0, theirs, mine)
            xg[c, s, zi, xi] = jnp.concatenate([top, bottom], axis=0).astype(BF)
        for s in ORDER:
            for d in range(1, nx):
                g1[s][d].start()

    ptw.wait_recv()
    piece = psend[...].astype(F32) + precv[...].astype(F32)
    gain_here = gain_ref[:, pl.ds(pl.multiple_of(chip * pc, 128), pc)]
    for k in range(2):
        scaled = piece[k] * gain_here if k == 0 else piece[k]
        wp[k, pl.ds(pl.multiple_of(ffw + g * 16, 16), 16), pl.ds(pl.multiple_of(chip * pc, 128), pc)] = scaled.astype(BF)

    def pref(group, first, width):
        return wp.at[c, pl.ds(pl.multiple_of(ffw + group * 16, 16), 16), pl.ds(pl.multiple_of(first * pc, 128), width * pc)]

    def psame(ref, i, j, dev):
        return rcopy(ref, ref, pp_s.at[i, j], pp_r.at[i, j], dev)

    px = [psame(pref(g, chip, 1), 0, d - 1, to_x(d)) for d in range(1, nx)]
    pz = [psame(pref(g, zi * nx, nx), 1, d - 1, to_z(d)) for d in range(1, nz)]
    py = [psame(pref(g, 0, nx * nz), 2, d - 1, to_y(d)) for d in range(1, ng)]
    fx = [psame(pref(g, zi * nx + xpeer(d), 1), 3, d - 1, twin) for d in range(1, nx)]
    fz = [psame(pref(g, zpeer(d) * nx, nx), 4, d - 1, twin) for d in range(1, nz)]
    fy = [psame(pref(lax.rem(g + d, ng), 0, nx * nz), 5, d - 1, twin) for d in range(1, ng)]
    sends.extend(px + pz + py + fx + fz + fy)

    def start(copies):
        for k in copies:
            k.start()

    def arrived(copies):
        for k in copies:
            k.wait_recv()

    start(px)

    def p_z():
        arrived(px)
        start(pz)
        start(fx)

    def p_y():
        arrived(pz)
        start(py)
        start(fz)

    def p_t():
        arrived(py)
        start(fy)

    def fold_gain():
        cw[0].wait()
        width = d_model // 12 if d_model % (12 * 128) == 0 else 128

        def part(j, carry):
            at = pl.ds(pl.multiple_of(j * width, 128), width)
            wp[0, 0:ffw, at] = (wp[0, 0:ffw, at].astype(F32) * gain_ref[:, at]).astype(BF)
            return carry

        lax.fori_loop(0, d_model // width, part, 0)

    @pl.when(sec == 1)
    def _():
        p_z()
        p_y()
        fold_gain()
        p_t()
        for s in range(STREAMS):
            g1[s][0].wait_recv()

    def second(s, d, e):
        ref = xg.at[c, s, zi, xfrom(d)] if s == A else xg.at[c, s, zfrom(d), xi]
        return rcopy(ref, ref, g2_s.at[s, e, d], g2_r.at[s, e, d], to_z(e) if s == A else to_x(e))

    def to_twin(s, d):
        ref = xg.at[c, s, zi, xfrom(d)] if s == A else xg.at[c, s, zfrom(d), xi]
        return rcopy(ref, ref, f1_s.at[s, d], f1_r.at[s, d], twin)

    g2 = {}
    f1, f2 = {}, {}

    def pass_on(s, d):
        for e in NEAR_FIRST:
            g2[s, d, e] = go(second(s, d, e))
        f1[s, d] = go(to_twin(s, d))

    for s in ORDER:
        pass_on(s, 0)

    @pl.when(sec == 0)
    def _():
        p_z()
        fold_gain()

    for d in NEAR_FIRST:
        for s in ORDER:
            g1[s][d].wait_recv()
            pass_on(s, d)

    @pl.when(sec == 0)
    def _():
        arrived(pz)
        start(fz)

        @pl.when(c == 0)
        def _():
            start(py)

    cw[1].wait()

    def up(h, s, total, ssq):
        lhs = xg[h, s].reshape(rows, sc)
        at = pl.ds(pl.multiple_of(h * hc + s * sc, 128), sc)
        wide = lhs.astype(F32)
        ssq = ssq + jnp.sum(wide * wide, axis=1, keepdims=True)
        part = lax.dot_general(lhs, wp[0, :, at], NT, preferred_element_type=F32)
        if total is None:
            acc[...] = part
        else:
            acc[...] += part
        return ssq

    for e in NEAR_FIRST:
        for s in ORDER:
            for d in range(nx):
                g2[s, d, e].wait_recv()
            ref = xg.at[c, s, zfrom(e)] if s == A else xg.at[c, s, :, xfrom(e)]
            f2[s, e] = go(rcopy(ref, ref, f2_s.at[s, e], f2_r.at[s, e], twin))
        if e == NEAR_FIRST[0]:

            @pl.when(sec == 0)
            def _():
                @pl.when(c == 1)
                def _():
                    start(py)

    @pl.when(sec == 0)
    def _():
        p_t()

    @pl.when(c == 1)
    def _():
        arrived(fx + fz + fy)

    ssq = jnp.zeros((rows, 1), F32)
    for n, s in enumerate(ORDER):
        ssq = up(c, s, None if n == 0 else acc, ssq)
    for s in ORDER:
        for d in range(nx):
            f1[s, d].wait_recv()
        for e in NEAR_FIRST:
            f2[s, e].wait_recv()
        ssq = up(o, s, acc, ssq)

    arrived(qsends)
    s_low = acc[:, ffw:]
    s_hi = s_low.astype(BF)
    s_lo = (s_low - s_hi.astype(F32)).astype(BF)
    q_up = qg[0].reshape(ng * 16, ffw)
    q_down = qg[1].reshape(ng * 16, ffw)
    low_rank = jnp.dot(s_hi, q_up, preferred_element_type=F32) + jnp.dot(s_lo, q_up, preferred_element_type=F32)
    row_scale = lax.rsqrt(ssq * (1.0 / d_model) + norm_eps)
    before = (acc[:, :ffw] + adapter_scale * low_rank) * row_scale
    valid = (lax.broadcasted_iota(jnp.int32, (rows, 1), 0) < len_ref[0]).astype(F32)
    hidden = (before / (1.0 + jnp.exp(-before)) * valid).astype(BF)
    hid[:, :ffw] = hidden
    hid[:, ffw:] = (adapter_scale * lax.dot_general(hidden, q_down, NT, preferred_element_type=F32)).astype(BF)

    @pl.when(c == 0)
    def _():
        arrived(fx + fz + fy)

    def down(h, s):
        at = pl.ds(pl.multiple_of(h * hc + s * sc, 128), sc)
        return jnp.dot(hid[...], wp[1, :, at], preferred_element_type=F32).astype(BF)

    rt = {}
    e1 = {}

    def twin_part(s):
        tsend[s] = down(o, s).reshape(nz, nx, 16, sc)
        rt[s] = go(rcopy(tsend.at[s], trecv.at[s], rt_s.at[s], rt_r.at[s], twin))

    def own_part(s):
        mine = down(c, s).reshape(nz, nx, 16, sc).astype(F32)
        rt[s].wait_recv()
        spart[s] = (mine + trecv[s].astype(F32)).astype(BF)
        for d in NEAR_FIRST:
            ref = spart.at[s, zpeer(d)] if s == A else spart.at[s, :, xpeer(d)]
            e1[s, d] = go(rcopy(ref, r1.at[s, d - 1], e1_s.at[s, d - 1], e1_r.at[s, d - 1], to_z(d) if s == A else to_x(d)))

    for n, s in enumerate(ORDER):
        twin_part(s)
        if n:
            own_part(ORDER[n - 1])
    own_part(ORDER[-1])

    e2 = {}
    for s in ORDER:
        total = spart[s, zi].astype(F32) if s == A else spart[s, :, xi].astype(F32)
        for d in NEAR_FIRST:
            e1[s, d].wait_recv()
            total = total + r1[s, d - 1].astype(F32)
        s1[s] = total.astype(BF)
        for d in NEAR_FIRST:
            peer = xpeer(d) if s == A else zpeer(d)
            e2[s, d] = go(rcopy(s1.at[s, peer], r2.at[s, d - 1], e2_s.at[s, d - 1], e2_r.at[s, d - 1], to_x(d) if s == A else to_z(d)))

    relay = []
    for s in ORDER:
        total = s1[s, xi if s == A else zi].astype(F32)
        for d in NEAR_FIRST:
            e2[s, d].wait_recv()
            total = total + r2[s, d - 1].astype(F32)
        total = total + xg[c, s, zi, xi].astype(F32)
        fb[s] = total.astype(BF)
        fs[0, :, s * sc:(s + 1) * sc] = total[:8]
        fs[1, :, s * sc:(s + 1) * sc] = total[8:]
        for d in range(nx):
            dev = {"section": 1, **(to_x(d) if s == A else to_z(d))}
            relay.append(rcopy(fb.at[s], own(s), rel_s.at[s, d], g1_r.at[s, d], dev))

        @pl.when(sec == 0)
        def _(s=s):
            start(relay[-nx:])

    fin = go(rcopy(fs.at[o], fr, bar_s.at[2], bar_r.at[2], twin))
    out_ref[0, :, mine_at] = fs[c].astype(BF)
    fin.wait_recv()
    out_ref[0, :, other_at] = fr[...].astype(BF)

    @pl.when(sec == 0)
    def _():
        xtw.wait_send()
        for s in range(STREAMS):
            for d in range(1, nx):
                g1[s][d].wait_send()
        for k in relay:
            k.wait_send()

    for k in sends:
        k.wait_send()


def body(inputs, lengths, norm_gain, base_weight, factor_p, factor_q):
    ng = lax.axis_size("group")
    nx = NX
    nz = lax.axis_size("tp") // 2 // nx
    assert nx == nz
    d_model = inputs.shape[1]
    ffw = base_weight.shape[3]
    rows = nz * nx * 16
    hc, pc = d_model // 2, d_model // (nz * nx)
    sc = hc // STREAMS
    vmem = pl.BlockSpec(memory_space=pltpu.VMEM)
    dma = pltpu.SemaphoreType.DMA
    n3 = max(nx, ng) - 1
    return pl.pallas_call(
        functools.partial(kernel, nz, nx, ng),
        out_shape=jax.ShapeDtypeStruct((1, 8, d_model), BF),
        in_specs=[
            vmem,
            pl.BlockSpec(memory_space=pltpu.SMEM),
            vmem,
            pl.BlockSpec(memory_space=pl.ANY),
            vmem,
            vmem,
        ],
        out_specs=vmem,
        scratch_shapes=[
            pltpu.VMEM((8, hc), F32),
            pltpu.VMEM((8, hc), F32),
            pltpu.VMEM((2, STREAMS, nz, nx, 16, sc), BF),
            pltpu.VMEM((2, ffw + ng * 16, d_model), BF),
            pltpu.VMEM((2, 16, pc), BF),
            pltpu.VMEM((2, 16, pc), BF),
            pltpu.VMEM((2, ng, 16, ffw), BF),
            pltpu.VMEM((rows, ffw + ng * 16), F32),
            pltpu.VMEM((rows, ffw + ng * 16), BF),
            pltpu.VMEM((STREAMS, nz, nx, 16, sc), BF),
            pltpu.VMEM((STREAMS, nz, nx, 16, sc), BF),
            pltpu.VMEM((STREAMS, nz, nx, 16, sc), BF),
            pltpu.VMEM((STREAMS, nx - 1, nx, 16, sc), BF),
            pltpu.VMEM((STREAMS, nx, 16, sc), BF),
            pltpu.VMEM((STREAMS, nx - 1, 16, sc), BF),
            pltpu.VMEM((STREAMS, 16, sc), BF),
            pltpu.VMEM((2, 8, hc), F32),
            pltpu.VMEM((8, hc), F32),
            dma((2,)),
            dma((3,)), dma((3,)),
            dma((STREAMS, nx)), dma((STREAMS, nx)),
            dma((STREAMS, nx, nx)), dma((STREAMS, nx, nx)),
            dma((STREAMS, nx)), dma((STREAMS, nx)),
            dma((STREAMS, nx)), dma((STREAMS, nx)),
            dma((6, n3)), dma((6, n3)),
            dma((1,)), dma((1,)),
            dma((n3,)), dma((n3,)),
            dma((STREAMS,)), dma((STREAMS,)),
            dma((STREAMS, nx)), dma((STREAMS, nx)),
            dma((STREAMS, nx)), dma((STREAMS, nx)),
            dma((STREAMS, nx)),
        ],
        compiler_params=pltpu.CompilerParams(
            collective_id=0, has_side_effects=True, vmem_limit_bytes=56 * 1024 * 1024
        ),
    )(inputs, lengths, norm_gain, jnp.swapaxes(base_weight[0], 1, 2), factor_p[0], factor_q[0])


def solution(mesh):
    return jax.shard_map(
        body,
        mesh=mesh,
        in_specs=(
            P(("group", "tp"), None),
            P("group"),
            P("section", None),
            P("section", None, None, "tp"),
            P("section", None, "group", "tp"),
            P("section", None, "group", "tp"),
        ),
        out_specs=P("section", ("group", "tp"), None),
        check_vma=False,
    )
```

```python
import functools

import jax
import jax.numpy as jnp
from jax import lax
from jax.experimental import pallas as pl
from jax.experimental.pallas import tpu as pltpu
from jax.sharding import PartitionSpec as P

adapter_scale = 2.0
norm_eps = 1e-05
NX = 4

BF, F32 = jnp.bfloat16, jnp.float32
NT = (((1,), (1,)), ((), ()))
STREAMS = 4
BLOCKS = ((0, 1), (2, 3))
GATHER_A, SCATTER_A = ((1, 3), ()), ((), (1, 3))
RELAYED_GATHER, RELAYED_SUM = ((0, 1, 2, 3),) * 2, ((0, 1, 2, 3),) * 2
NEAR_FIRST = (1, 3, 2)
PIECES = (0, 1, 3, 2)


def kernel(
    nz, nx, ng,
    x_ref, len_ref, gain_ref, w_ref, p_ref, q_ref,
    out_ref,
    xs, xt, xg, wp, psend, precv, qg, acc, hid, tsend, trecv, spart, far, r1, s1, r2, fb, fs, fr, low_send, low_recv, u_send, u_recv,
    wsem, bar_s, bar_r, g1_s, g1_r, g2_s, g2_r, f1_s, f1_r, f2_s, f2_r,
    pz_s, pz_r, px_s, px_r, py_s, py_r, low_s, low_r, qy_s, qy_r, rt_s, rt_r, e1_s, e1_r, e2_s, e2_r, rel_s,
):
    g = lax.axis_index("group")
    sec = lax.axis_index("section")
    t = lax.axis_index("tp")
    c = lax.rem(t, 2)
    o = 1 - c
    chip = lax.div(t, 2)
    xi = lax.rem(chip, nx)
    zi = lax.div(chip, nx)
    d_model = x_ref.shape[1]
    ffw = w_ref.shape[1]
    hc = d_model // 2
    kc = hc // 2
    sc = kc // 2
    chips = nz * nx
    rows = chips * 8
    pc = d_model // chips

    def tp_of(z, x, core):
        return (z * nx + x) * 2 + core

    xpeers = [lax.rem(xi + d, nx) for d in range(nx)]
    zpeers = [lax.rem(zi + d, nz) for d in range(nz)]
    xfroms = [lax.rem(xi + nx - d, nx) for d in range(nx)]
    zfroms = [lax.rem(zi + nz - d, nz) for d in range(nz)]
    twin = {"tp": tp_of(zi, xi, o)}
    to_x = [{"tp": tp_of(zi, xpeers[d], c)} for d in range(nx)]
    to_z = [{"tp": tp_of(zpeers[d], xi, c)} for d in range(nz)]
    to_y = [{"group": lax.rem(g + d, ng)} for d in range(ng)]
    sec0, sec1 = sec == 0, sec == 1

    def rcopy(src, dst, ss, rs, dev):
        return pltpu.make_async_remote_copy(
            src_ref=src, dst_ref=dst, send_sem=ss, recv_sem=rs,
            device_id=dev, device_id_type=pl.DeviceIdType.MESH,
        )

    def start(copies):
        for k in copies:
            k.start()

    def arrived(copies):
        for k in copies:
            k.wait_recv()

    cw = [pltpu.make_async_copy(w_ref.at[k], wp.at[k, 0:ffw], wsem.at[k]) for k in range(2)]
    start(cw)

    barrier = pltpu.get_barrier_semaphore()
    peers = [twin, *to_x[1:], *to_z[1:], *to_y[1:], {"section": 1 - sec}]
    peers += [{"section": 1 - sec, **dev} for dev in to_x[1:] + to_z[1:]]
    for dev in peers:
        pl.semaphore_signal(barrier, inc=1, device_id=dev, device_id_type=pl.DeviceIdType.MESH)

    pf = p_ref[...].astype(F32)
    blank = jnp.zeros_like(pf)
    psend[...] = jnp.where(
        c == 0, jnp.concatenate([pf, blank], axis=2), jnp.concatenate([blank, pf], axis=2)
    ).astype(BF)
    mine_at = pl.ds(pl.multiple_of(c * hc, 128), hc)
    other_at = pl.ds(pl.multiple_of(o * hc, 128), hc)
    xs[...] = x_ref[:, other_at].astype(F32)
    qg[:, g] = q_ref[...]

    xtw = rcopy(xs, xt, bar_s.at[0], bar_r.at[0], twin)
    ptw = rcopy(psend, precv, bar_s.at[1], bar_r.at[1], twin)
    qsends = [rcopy(q_ref, qg.at[:, g], qy_s.at[d - 1], qy_r.at[d - 1], to_y[d]) for d in range(1, ng)]

    zh = nz // 2
    is_source = lax.div(zi, zh) == c

    def p_rows(group):
        return pl.ds(pl.multiple_of(ffw + group * 16, 16), 16)

    def p_piece(m):
        return wp.at[:, p_rows(g), pl.ds(pl.multiple_of(((c * zh + m) * nx + xi) * pc, 128), pc)]

    mine = lax.rem(zi, zh)
    pz = [rcopy(p_piece(mine), p_piece(mine), pz_s.at[d - 1], pz_r.at[mine], to_z[d]) for d in range(1, nz)]
    pz_in = [rcopy(p_piece(m), p_piece(m), pz_s.at[0], pz_r.at[m], to_z[1]) for m in range(zh)]
    px = [
        rcopy(p_piece(m), p_piece(m), px_s.at[d - 1, m], px_r.at[d - 1, m], to_x[d])
        for d in range(1, nx) for m in range(zh)
    ]
    py = [[], []]
    for k in range(2):
        ref = wp.at[k, p_rows(g), mine_at]
        py[k] = [rcopy(ref, ref, py_s.at[k, e - 1], py_r.at[k, e - 1], to_y[e]) for e in range(1, ng)]

    def p_z():
        @pl.when(is_source)
        def _():
            start(pz)

    def p_x():
        for m in range(zh):
            @pl.when(zi != c * zh + m)
            def _(m=m):
                pz_in[m].wait_recv()

        start(px)

    def p_y():
        arrived(px)
        start(py[0] + py[1])

    pl.semaphore_wait(barrier, len(peers))

    @pl.when(sec0)
    def _():
        xtw.start()

    ptw.start()
    start(qsends)

    ptw.wait_recv()
    piece = psend[...].astype(F32) + precv[...].astype(F32)
    gain_here = gain_ref[:, pl.ds(pl.multiple_of(chip * pc, 128), pc)]
    for k in range(2):
        scaled = piece[k] * gain_here if k == 0 else piece[k]
        wp[k, pl.ds(pl.multiple_of(ffw + g * 16, 16), 16), pl.ds(pl.multiple_of(chip * pc, 128), pc)] = scaled.astype(BF)
    p_z()

    def fold_gain():
        cw[0].wait()
        width = d_model // 12 if d_model % (12 * 128) == 0 else 128

        def fold(j, carry):
            at = pl.ds(pl.multiple_of(j * width, 128), width)
            wp[0, 0:ffw, at] = (wp[0, 0:ffw, at].astype(F32) * gain_ref[:, at]).astype(BF)
            return carry

        lax.fori_loop(0, d_model // width, fold, 0)

    def run(layer):
        sends = [ptw, *qsends, *px, *py[0], *py[1]]

        def kept(copy):
            sends.append(copy)
            return copy

        def go(copy):
            copy.start()
            return kept(copy)

        ga, sa = GATHER_A[layer], SCATTER_A[layer]

        def at_first(s, d):
            return xg.at[c, s, zi, xfroms[d]] if s in ga else xg.at[c, s, zfroms[d], xi]

        def at_both(s, d, e):
            return xg.at[c, s, zfroms[e], xfroms[d]] if s in ga else xg.at[c, s, zfroms[d], xfroms[e]]

        def first_axis(s, d, a=ga):
            return to_x[d] if s in a else to_z[d]

        def second_axis(s, d, a=ga):
            return to_z[d] if s in a else to_x[d]

        def way(s, d):
            if s in ga:
                return 1 if d == 2 else 3
            return 1 if d in (0, 3) else 3

        g1, g2, g3, f1, f2 = {}, {}, {}, {}, {}
        for s in range(STREAMS):
            for d in range(nx):
                ref = at_first(s, 0)
                g1[s, d] = rcopy(ref, ref, g1_s.at[s, d], g1_r.at[s, d], first_axis(s, d))
                ref = at_first(s, d)
                for e in (1, 3):
                    g2[s, d, e] = kept(rcopy(ref, ref, g2_s.at[s, e, d], g2_r.at[s, e, d], second_axis(s, e)))
                f1[s, d] = kept(rcopy(ref, ref, f1_s.at[s, d], f1_r.at[s, d], twin))
                if s in RELAYED_GATHER[layer]:
                    e = way(s, d)
                    ref = at_both(s, d, e)
                else:
                    e = 2
                g3[s, d] = kept(rcopy(ref, ref, g2_s.at[s, 2, d], g2_r.at[s, 2, d], second_axis(s, e)))
            for e in (1, 3, 2):
                ref = xg.at[c, s, zfroms[e]] if s in ga else xg.at[c, s, :, xfroms[e]]
                f2[s, e] = kept(rcopy(ref, ref, f2_s.at[s, e], f2_r.at[s, e], twin))

        def pass_on(s, d):
            start((g2[s, d, way(s, d)], g2[s, d, 4 - way(s, d)], f1[s, d]))
            if s not in RELAYED_GATHER[layer]:
                g3[s, d].start()

        def gather_first(b):
            for d in NEAR_FIRST:
                for s in BLOCKS[b]:
                    g1[s, d].wait_recv()
                    pass_on(s, d)

        def gather_second(b):
            for d in PIECES:
                for s in BLOCKS[b]:
                    for e in (way(s, d), 4 - way(s, d)):
                        g2[s, d, e].wait_recv()
                        if e == way(s, d) and s in RELAYED_GATHER[layer]:
                            g3[s, d].start()
            for s in BLOCKS[b]:
                start((f2[s, 1], f2[s, 3]))

        def gather_far(b):
            for s in BLOCKS[b]:
                for d in PIECES:
                    g3[s, d].wait_recv()
                f2[s, 2].start()

        def own_pieces(b):
            for s in BLOCKS[b]:
                k = s % 2
                mine = x_ref[:, pl.ds(pl.multiple_of(c * hc + k * kc, 128), kc)].astype(F32)
                piece = jnp.where(c == b, mine, xt[:, k * kc:(k + 1) * kc])
                xg[c, s, zi, xi] = jnp.concatenate([piece[:, :sc], piece[:, sc:]], axis=0).astype(BF)

        def send_first(b):
            for d in NEAR_FIRST:
                for s in BLOCKS[b]:
                    g1[s, d].start()

        if layer == 0:
            xtw.wait_recv()
            own_pieces(0)
            send_first(0)
            own_pieces(1)
            for s in BLOCKS[0]:
                pass_on(s, 0)
            send_first(1)
            fold_gain()
            p_x()
            for s in BLOCKS[1]:
                pass_on(s, 0)
            gather_first(0)
            p_y()
            gather_first(1)
            gather_second(0)
            gather_second(1)
        else:
            fold_gain()
            p_x()
            p_y()
            for b in range(2):
                for s in BLOCKS[b]:
                    g1[s, 0].wait_recv()
                    pass_on(s, 0)
                gather_first(b)
                if b == 0:
                    gather_second(0)

        cw[1].wait()
        valid_to = len_ref[0]

        def columns(h, s, f):
            return pl.ds(pl.multiple_of(h * hc + s % 2 * kc + f * sc, 128), sc)

        def up(h, s, ssq, first):
            wide = xg[h, s].reshape(chips, 16, sc).astype(F32)
            for f in range(2):
                lhs = wide[:, f * 8:(f + 1) * 8].reshape(rows, sc)
                ssq = ssq + jnp.sum(lhs * lhs, axis=1, keepdims=True)
                lhs = lhs.astype(BF)
                if h is c:
                    part = lax.dot_general(lhs, wp[0, :, columns(h, s, f)], NT, preferred_element_type=F32)
                    if first and f == 0:
                        acc[...] = part
                    else:
                        acc[...] += part
                else:
                    acc[:, :ffw] += lax.dot_general(lhs, wp[0, 0:ffw, columns(h, s, f)], NT, preferred_element_type=F32)
            return ssq

        def up_block(b):
            gather_far(b)
            if b == 0:
                arrived(py[0])
            ssq = jnp.zeros((rows, 1), F32)
            for n, s in enumerate(BLOCKS[b]):
                ssq = up(c, s, ssq, n == 0)
            low_send[b] = acc[:, ffw:]
            low = go(rcopy(low_send.at[b], low_recv.at[b], low_s.at[0, b], low_r.at[0, b], twin))
            for s in BLOCKS[b]:
                arrived([f1[s, d] for d in range(nx)] + [f2[s, e] for e in (1, 3, 2)])
                ssq = up(o, s, ssq, False)
            if b == 0:
                arrived(qsends)
            low.wait_recv()
            s_low = low_send[b] + low_recv[b]
            s_hi = s_low.astype(BF)
            s_lo = (s_low - s_hi.astype(F32)).astype(BF)
            q_up = qg[0].reshape(ng * 16, ffw)
            q_down = qg[1].reshape(ng * 16, ffw)
            low_rank = jnp.dot(s_hi, q_up, preferred_element_type=F32) + jnp.dot(s_lo, q_up, preferred_element_type=F32)
            row_scale = lax.rsqrt(ssq * (1.0 / d_model) + norm_eps)
            before = (acc[:, :ffw] + adapter_scale * low_rank) * row_scale
            r = lax.broadcasted_iota(jnp.int32, (rows, 1), 0)
            position = (r - (r & 7)) * 2 + b * 8 + (r & 7)
            valid = (position < valid_to).astype(F32)
            hidden = (before / (1.0 + jnp.exp(-before)) * valid).astype(BF)
            hid[:, :ffw] = hidden
            u_send[b] = adapter_scale * lax.dot_general(hidden, q_down, NT, preferred_element_type=F32)

        def down(h, s):
            n = ffw + ng * 16 if h is c else ffw
            parts = [
                jnp.dot(hid[:, :n], wp[1, 0:n, columns(h, s, f)], preferred_element_type=F32).reshape(chips, 8, sc)
                for f in range(2)
            ]
            return jnp.concatenate(parts, axis=1).astype(BF).reshape(nz, nx, 16, sc)

        rt, e1, e2 = {}, {}, {}

        def part(s, peer, lo, hi):
            return spart.at[s, peer, lo:hi] if s in sa else spart.at[s, lo:hi, peer]

        def peer_of(s, d):
            return zpeers[d] if s in sa else xpeers[d]

        def split(s):
            return 1 if s in sa else nx // 2

        def twin_part(s):
            tsend[s] = down(o, s)
            rt[s] = go(rcopy(tsend.at[s], trecv.at[s], rt_s.at[s], rt_r.at[s], twin))

        def own_part(s):
            mine = down(c, s).astype(F32)
            rt[s].wait_recv()
            spart[s] = (mine + trecv[s].astype(F32)).astype(BF)
            m = split(s)

            def put(i, ref, dst, d):
                e1[s, i] = go(rcopy(ref, dst, e1_s.at[s, i], e1_r.at[s, i], second_axis(s, d, sa)))

            if s not in RELAYED_SUM[layer]:
                put(2, part(s, peer_of(s, 1), 0, nx), r1.at[s, 0], 1)
                put(3, part(s, peer_of(s, 3), 0, nx), r1.at[s, 1], 3)
                put(4, part(s, peer_of(s, 2), 0, nx), far.at[s], 2)
                return
            put(0, part(s, peer_of(s, 2), 0, m), far.at[s, 0:m], 1)
            put(1, part(s, peer_of(s, 2), m, nx), far.at[s, m:nx], 3)
            put(2, part(s, peer_of(s, 1), m, nx), r1.at[s, 0, m:nx], 1)
            put(3, part(s, peer_of(s, 3), 0, m), r1.at[s, 1, 0:m], 3)

        def sum_part(s):
            m = split(s)
            for i, d, lo, hi in ((0, 1, 0, m), (1, 3, m, nx)):
                e1[s, i].wait_recv()
                far[s, lo:hi] = (far[s, lo:hi].astype(F32) + part(s, peer_of(s, d), lo, hi)[...].astype(F32)).astype(BF)
                e1[s, 4 + i] = go(rcopy(far.at[s, lo:hi], r1.at[s, i, lo:hi], e1_s.at[s, 4 + i], e1_r.at[s, 4 + i], second_axis(s, d, sa)))

        def down_block(b):
            u = go(rcopy(u_send.at[b], u_recv.at[b], low_s.at[1, b], low_r.at[1, b], twin))
            for s in BLOCKS[b]:
                twin_part(s)
            u.wait_recv()
            hid[:, ffw:] = (u_send[b] + u_recv[b]).astype(BF)
            if b == 0:
                arrived(py[1])
            for s in BLOCKS[b]:
                own_part(s)

        def sum_block(b):
            for s in BLOCKS[b]:
                if s in RELAYED_SUM[layer]:
                    sum_part(s)

        def scatter_second(b):
            for s in BLOCKS[b]:
                for i in range(2, 6 if s in RELAYED_SUM[layer] else 5):
                    e1[s, i].wait_recv()
                total = spart[s, zi].astype(F32) if s in sa else spart[s, :, xi].astype(F32)
                total = total + r1[s, 0].astype(F32) + r1[s, 1].astype(F32)
                if s not in RELAYED_SUM[layer]:
                    total = total + far[s].astype(F32)
                s1[s] = total.astype(BF)
                for d in NEAR_FIRST:
                    peer = xpeers[d] if s in sa else zpeers[d]
                    e2[s, d] = go(rcopy(s1.at[s, peer], r2.at[s, d - 1], e2_s.at[s, d - 1], e2_r.at[s, d - 1], first_axis(s, d, sa)))

        relay = []

        def finish(b):
            for s in BLOCKS[b]:
                k = s % 2
                total = s1[s, xi if s in sa else zi].astype(F32)
                for d in NEAR_FIRST:
                    e2[s, d].wait_recv()
                    total = total + r2[s, d - 1].astype(F32)
                total = total + xg[c, s, zi, xi].astype(F32)
                fb[s] = total.astype(BF)
                fs[b, :, k * kc:k * kc + sc] = total[:8]
                fs[b, :, k * kc + sc:(k + 1) * kc] = total[8:]
                if layer:
                    continue
                here = [
                    rcopy(fb.at[s], at_first(s, 0), rel_s.at[s, d], g1_r.at[s, d], {"section": 1, **first_axis(s, d, GATHER_A[1])})
                    for d in range(nx)
                ]
                relay.extend(here)
                start(here)

        up_block(0)
        if layer == 1:
            gather_second(1)
        down_block(0)
        up_block(1)
        sum_block(0)
        down_block(1)
        scatter_second(0)
        sum_block(1)
        finish(0)
        scatter_second(1)
        finish(1)

        fin = go(rcopy(fs.at[o], fr, bar_s.at[2], bar_r.at[2], twin))
        out_ref[0, :, mine_at] = fs[c].astype(BF)
        fin.wait_recv()
        out_ref[0, :, other_at] = fr[...].astype(BF)
        if layer == 0:
            sends.append(xtw)
            sends.extend(g1[s, d] for s in range(STREAMS) for d in range(1, nx))
        @pl.when(is_source)
        def _():
            for k in pz:
                k.wait_send()

        for k in sends + relay:
            k.wait_send()

    @pl.when(sec0)
    def _():
        run(0)

    @pl.when(sec1)
    def _():
        run(1)


def body(inputs, lengths, norm_gain, base_weight, factor_p, factor_q):
    ng = lax.axis_size("group")
    nx = NX
    nz = lax.axis_size("tp") // 2 // nx
    assert nx == nz
    d_model = inputs.shape[1]
    ffw = base_weight.shape[3]
    rows = nz * nx * 8
    hc, pc = d_model // 2, d_model // (nz * nx)
    sc = hc // STREAMS
    vmem = pl.BlockSpec(memory_space=pltpu.VMEM)
    dma = pltpu.SemaphoreType.DMA
    n3 = max(nx, ng) - 1
    return pl.pallas_call(
        functools.partial(kernel, nz, nx, ng),
        out_shape=jax.ShapeDtypeStruct((1, 8, d_model), BF),
        in_specs=[
            vmem,
            pl.BlockSpec(memory_space=pltpu.SMEM),
            vmem,
            pl.BlockSpec(memory_space=pl.ANY),
            vmem,
            vmem,
        ],
        out_specs=vmem,
        scratch_shapes=[
            pltpu.VMEM((8, hc), F32),
            pltpu.VMEM((8, hc), F32),
            pltpu.VMEM((2, STREAMS, nz, nx, 16, sc), BF),
            pltpu.VMEM((2, ffw + ng * 16, d_model), BF),
            pltpu.VMEM((2, 16, pc), BF),
            pltpu.VMEM((2, 16, pc), BF),
            pltpu.VMEM((2, ng, 16, ffw), BF),
            pltpu.VMEM((rows, ffw + ng * 16), F32),
            pltpu.VMEM((rows, ffw + ng * 16), BF),
            pltpu.VMEM((STREAMS, nz, nx, 16, sc), BF),
            pltpu.VMEM((STREAMS, nz, nx, 16, sc), BF),
            pltpu.VMEM((STREAMS, nz, nx, 16, sc), BF),
            pltpu.VMEM((STREAMS, nx, 16, sc), BF),
            pltpu.VMEM((STREAMS, 2, nx, 16, sc), BF),
            pltpu.VMEM((STREAMS, nx, 16, sc), BF),
            pltpu.VMEM((STREAMS, nx - 1, 16, sc), BF),
            pltpu.VMEM((STREAMS, 16, sc), BF),
            pltpu.VMEM((2, 8, hc), F32),
            pltpu.VMEM((8, hc), F32),
            pltpu.VMEM((2, rows, ng * 16), F32),
            pltpu.VMEM((2, rows, ng * 16), F32),
            pltpu.VMEM((2, rows, ng * 16), F32),
            pltpu.VMEM((2, rows, ng * 16), F32),
            dma((2,)),
            dma((3,)), dma((3,)),
            dma((STREAMS, nx)), dma((STREAMS, nx)),
            dma((STREAMS, nx, nx)), dma((STREAMS, nx, nx)),
            dma((STREAMS, nx)), dma((STREAMS, nx)),
            dma((STREAMS, nx)), dma((STREAMS, nx)),
            dma((n3,)), dma((n3,)),
            dma((n3, nz // 2)), dma((n3, nz // 2)),
            dma((2, n3)), dma((2, n3)),
            dma((2, 2)), dma((2, 2)),
            dma((n3,)), dma((n3,)),
            dma((STREAMS,)), dma((STREAMS,)),
            dma((STREAMS, 6)), dma((STREAMS, 6)),
            dma((STREAMS, nx)), dma((STREAMS, nx)),
            dma((STREAMS, nx)),
        ],
        compiler_params=pltpu.CompilerParams(
            collective_id=0, has_side_effects=True, vmem_limit_bytes=56 * 1024 * 1024
        ),
    )(inputs, lengths, norm_gain, jnp.swapaxes(base_weight[0], 1, 2), factor_p[0], factor_q[0])


def solution(mesh):
    return jax.shard_map(
        body,
        mesh=mesh,
        in_specs=(
            P(("group", "tp"), None),
            P("group"),
            P("section", None),
            P("section", None, None, "tp"),
            P("section", None, "group", "tp"),
            P("section", None, "group", "tp"),
        ),
        out_specs=P("section", ("group", "tp"), None),
        check_vma=False,
    )
```

```python
import functools

import jax
import jax.numpy as jnp
from jax import lax
from jax.experimental import pallas as pl
from jax.experimental.pallas import tpu as pltpu
from jax.sharding import PartitionSpec as P

adapter_scale = 2.0
norm_eps = 1e-05
NX = 4

BF, F32 = jnp.bfloat16, jnp.float32
NT = (((1,), (1,)), ((), ()))
STREAMS = 4
BLOCKS = ((0, 1), (2, 3))
GATHER_A, SCATTER_A = ((1, 3), ()), ((), (1, 3))
RELAYED_GATHER, RELAYED_SUM = ((0, 1, 2, 3),) * 2, ((0, 1, 2, 3),) * 2
NEAR_FIRST = (1, 3, 2)
PIECES = (0, 1, 3, 2)


def kernel(
    nz, nx, ng,
    x_ref, len_ref, gain_ref, w_ref, p_ref, q_ref,
    out_ref,
    xs, xt, xg, wp, psend, precv, qg, acc, hid, tsend, trecv, spart, far, r1, s1, r2, fb, fs, fr, low_send, low_recv, u_send, u_recv,
    wsem, bar_s, bar_r, g1_s, g1_r, g2_s, g2_r, f1_s, f1_r, f2_s, f2_r,
    pz_s, pz_r, px_s, px_r, py_s, py_r, low_s, low_r, qy_s, qy_r, rt_s, rt_r, e1_s, e1_r, e2_s, e2_r, rel_s,
):
    g = lax.axis_index("group")
    sec = lax.axis_index("section")
    t = lax.axis_index("tp")
    c = lax.rem(t, 2)
    o = 1 - c
    chip = lax.div(t, 2)
    xi = lax.rem(chip, nx)
    zi = lax.div(chip, nx)
    d_model = x_ref.shape[1]
    ffw = w_ref.shape[1]
    hc = d_model // 2
    kc = hc // 2
    sc = kc // 2
    chips = nz * nx
    rows = chips * 8
    pc = d_model // chips

    def tp_of(z, x, core):
        return (z * nx + x) * 2 + core

    xpeers = [lax.rem(xi + d, nx) for d in range(nx)]
    zpeers = [lax.rem(zi + d, nz) for d in range(nz)]
    xfroms = [lax.rem(xi + nx - d, nx) for d in range(nx)]
    zfroms = [lax.rem(zi + nz - d, nz) for d in range(nz)]
    twin = {"tp": tp_of(zi, xi, o)}
    to_x = [{"tp": tp_of(zi, xpeers[d], c)} for d in range(nx)]
    to_z = [{"tp": tp_of(zpeers[d], xi, c)} for d in range(nz)]
    to_y = [{"group": lax.rem(g + d, ng)} for d in range(ng)]
    sec0, sec1 = sec == 0, sec == 1

    def rcopy(src, dst, ss, rs, dev):
        return pltpu.make_async_remote_copy(
            src_ref=src, dst_ref=dst, send_sem=ss, recv_sem=rs,
            device_id=dev, device_id_type=pl.DeviceIdType.MESH,
        )

    def start(copies):
        for k in copies:
            k.start()

    def arrived(copies):
        for k in copies:
            k.wait_recv()

    cw = [pltpu.make_async_copy(w_ref.at[k], wp.at[k, 0:ffw], wsem.at[k]) for k in range(2)]
    start(cw)

    barrier = pltpu.get_barrier_semaphore()
    peers = [twin, *to_x[1:], *to_z[1:], *to_y[1:], {"section": 1 - sec}]
    peers += [{"section": 1 - sec, **dev} for dev in to_x[1:] + to_z[1:]]
    for dev in peers:
        pl.semaphore_signal(barrier, inc=1, device_id=dev, device_id_type=pl.DeviceIdType.MESH)

    pf = p_ref[...].astype(F32)
    blank = jnp.zeros_like(pf)
    psend[...] = jnp.where(
        c == 0, jnp.concatenate([pf, blank], axis=2), jnp.concatenate([blank, pf], axis=2)
    ).astype(BF)
    mine_at = pl.ds(pl.multiple_of(c * hc, 128), hc)
    other_at = pl.ds(pl.multiple_of(o * hc, 128), hc)
    xs[...] = x_ref[:, other_at].astype(F32)
    qg[:, g] = q_ref[...]

    xtw = rcopy(xs, xt, bar_s.at[0], bar_r.at[0], twin)
    ptw = rcopy(psend, precv, bar_s.at[1], bar_r.at[1], twin)
    qsends = [rcopy(q_ref, qg.at[:, g], qy_s.at[d - 1], qy_r.at[d - 1], to_y[d]) for d in range(1, ng)]

    zh = nz // 2
    is_source = lax.div(zi, zh) == c

    def p_rows(group):
        return pl.ds(pl.multiple_of(ffw + group * 16, 16), 16)

    def p_piece(m):
        return wp.at[:, p_rows(g), pl.ds(pl.multiple_of(((c * zh + m) * nx + xi) * pc, 128), pc)]

    mine = lax.rem(zi, zh)
    pz = [rcopy(p_piece(mine), p_piece(mine), pz_s.at[d - 1], pz_r.at[mine], to_z[d]) for d in range(1, nz)]
    pz_in = [rcopy(p_piece(m), p_piece(m), pz_s.at[0], pz_r.at[m], to_z[1]) for m in range(zh)]
    px = [
        rcopy(p_piece(m), p_piece(m), px_s.at[d - 1, m], px_r.at[d - 1, m], to_x[d])
        for d in range(1, nx) for m in range(zh)
    ]
    py = [[], []]
    for k in range(2):
        ref = wp.at[k, p_rows(g), mine_at]
        py[k] = [rcopy(ref, ref, py_s.at[k, e - 1], py_r.at[k, e - 1], to_y[e]) for e in range(1, ng)]

    def p_z():
        @pl.when(is_source)
        def _():
            start(pz)

    def p_x():
        for m in range(zh):
            @pl.when(zi != c * zh + m)
            def _(m=m):
                pz_in[m].wait_recv()

        start(px)

    def p_y():
        arrived(px)
        start(py[0] + py[1])

    pl.semaphore_wait(barrier, len(peers))

    @pl.when(sec0)
    def _():
        xtw.start()

    ptw.start()
    start(qsends)

    ptw.wait_recv()
    piece = psend[...].astype(F32) + precv[...].astype(F32)
    gain_here = gain_ref[:, pl.ds(pl.multiple_of(chip * pc, 128), pc)]
    for k in range(2):
        scaled = piece[k] * gain_here if k == 0 else piece[k]
        wp[k, pl.ds(pl.multiple_of(ffw + g * 16, 16), 16), pl.ds(pl.multiple_of(chip * pc, 128), pc)] = scaled.astype(BF)
    p_z()

    def fold_gain():
        cw[0].wait()
        width = d_model // 12 if d_model % (12 * 128) == 0 else 128

        def fold(j, carry):
            at = pl.ds(pl.multiple_of(j * width, 128), width)
            wp[0, 0:ffw, at] = (wp[0, 0:ffw, at].astype(F32) * gain_ref[:, at]).astype(BF)
            return carry

        lax.fori_loop(0, d_model // width, fold, 0)

    def run(layer):
        sends = [ptw, *qsends, *px, *py[0], *py[1]]

        def kept(copy):
            sends.append(copy)
            return copy

        def go(copy):
            copy.start()
            return kept(copy)

        ga, sa = GATHER_A[layer], SCATTER_A[layer]

        def at_first(s, d):
            return xg.at[c, s, zi, xfroms[d]] if s in ga else xg.at[c, s, zfroms[d], xi]

        def at_both(s, d, e):
            return xg.at[c, s, zfroms[e], xfroms[d]] if s in ga else xg.at[c, s, zfroms[d], xfroms[e]]

        def first_axis(s, d, a=ga):
            return to_x[d] if s in a else to_z[d]

        def second_axis(s, d, a=ga):
            return to_z[d] if s in a else to_x[d]

        def way(s, d):
            if s in ga:
                return 1 if d == 2 else 3
            return 1 if d in (0, 3) else 3

        g1, g2, g3, f1, f2 = {}, {}, {}, {}, {}
        for s in range(STREAMS):
            for d in range(nx):
                ref = at_first(s, 0)
                g1[s, d] = rcopy(ref, ref, g1_s.at[s, d], g1_r.at[s, d], first_axis(s, d))
                ref = at_first(s, d)
                for e in (1, 3):
                    g2[s, d, e] = kept(rcopy(ref, ref, g2_s.at[s, e, d], g2_r.at[s, e, d], second_axis(s, e)))
                f1[s, d] = kept(rcopy(ref, ref, f1_s.at[s, d], f1_r.at[s, d], twin))
                if s in RELAYED_GATHER[layer]:
                    e = way(s, d)
                    ref = at_both(s, d, e)
                else:
                    e = 2
                g3[s, d] = kept(rcopy(ref, ref, g2_s.at[s, 2, d], g2_r.at[s, 2, d], second_axis(s, e)))
            for e in (1, 3, 2):
                ref = xg.at[c, s, zfroms[e]] if s in ga else xg.at[c, s, :, xfroms[e]]
                f2[s, e] = kept(rcopy(ref, ref, f2_s.at[s, e], f2_r.at[s, e], twin))

        def pass_on(s, d):
            start((g2[s, d, way(s, d)], g2[s, d, 4 - way(s, d)], f1[s, d]))
            if s not in RELAYED_GATHER[layer]:
                g3[s, d].start()

        def gather_first(b):
            for d in NEAR_FIRST:
                for s in BLOCKS[b]:
                    g1[s, d].wait_recv()
                    pass_on(s, d)

        def gather_second(b):
            for d in PIECES:
                for s in BLOCKS[b]:
                    for e in (way(s, d), 4 - way(s, d)):
                        g2[s, d, e].wait_recv()
                        if e == way(s, d) and s in RELAYED_GATHER[layer]:
                            g3[s, d].start()
            for s in BLOCKS[b]:
                start((f2[s, 1], f2[s, 3]))

        def gather_far(b):
            for s in BLOCKS[b]:
                for d in PIECES:
                    g3[s, d].wait_recv()
                f2[s, 2].start()

        def own_pieces(b):
            for s in BLOCKS[b]:
                k = s % 2
                mine = x_ref[:, pl.ds(pl.multiple_of(c * hc + k * kc, 128), kc)].astype(F32)
                piece = jnp.where(c == b, mine, xt[:, k * kc:(k + 1) * kc])
                xg[c, s, zi, xi] = jnp.concatenate([piece[:, :sc], piece[:, sc:]], axis=0).astype(BF)

        def send_first(b):
            for d in NEAR_FIRST:
                for s in BLOCKS[b]:
                    g1[s, d].start()

        if layer == 0:
            xtw.wait_recv()
            own_pieces(0)
            send_first(0)
            own_pieces(1)
            for s in BLOCKS[0]:
                pass_on(s, 0)
            send_first(1)
            fold_gain()
            p_x()
            for s in BLOCKS[1]:
                pass_on(s, 0)
            gather_first(0)
            p_y()
            gather_first(1)
            gather_second(0)
            gather_second(1)
        else:
            fold_gain()
            p_x()
            p_y()
            for b in range(2):
                for s in BLOCKS[b]:
                    g1[s, 0].wait_recv()
                    pass_on(s, 0)
                gather_first(b)
                if b == 0:
                    gather_second(0)

        cw[1].wait()
        valid_to = len_ref[0]

        def columns(h, s, f):
            return pl.ds(pl.multiple_of(h * hc + s % 2 * kc + f * sc, 128), sc)

        def up(h, s, ssq, first):
            wide = xg[h, s].reshape(chips, 16, sc).astype(F32)
            for f in range(2):
                lhs = wide[:, f * 8:(f + 1) * 8].reshape(rows, sc)
                ssq = ssq + jnp.sum(lhs * lhs, axis=1, keepdims=True)
                lhs = lhs.astype(BF)
                if h is c:
                    part = lax.dot_general(lhs, wp[0, :, columns(h, s, f)], NT, preferred_element_type=F32)
                    if first and f == 0:
                        acc[...] = part
                    else:
                        acc[...] += part
                else:
                    acc[:, :ffw] += lax.dot_general(lhs, wp[0, 0:ffw, columns(h, s, f)], NT, preferred_element_type=F32)
            return ssq

        def up_block(b):
            gather_far(b)
            if b == 0:
                arrived(py[0])
            ssq = jnp.zeros((rows, 1), F32)
            for n, s in enumerate(BLOCKS[b]):
                ssq = up(c, s, ssq, n == 0)
            low_send[b] = acc[:, ffw:]
            low = go(rcopy(low_send.at[b], low_recv.at[b], low_s.at[0, b], low_r.at[0, b], twin))
            for s in BLOCKS[b]:
                arrived([f1[s, d] for d in range(nx)] + [f2[s, e] for e in (1, 3, 2)])
                ssq = up(o, s, ssq, False)
            if b == 0:
                arrived(qsends)
            low.wait_recv()
            s_low = low_send[b] + low_recv[b]
            s_hi = s_low.astype(BF)
            s_lo = (s_low - s_hi.astype(F32)).astype(BF)
            q_up = qg[0].reshape(ng * 16, ffw)
            q_down = qg[1].reshape(ng * 16, ffw)
            low_rank = jnp.dot(s_hi, q_up, preferred_element_type=F32) + jnp.dot(s_lo, q_up, preferred_element_type=F32)
            row_scale = lax.rsqrt(ssq * (1.0 / d_model) + norm_eps)
            before = (acc[:, :ffw] + adapter_scale * low_rank) * row_scale
            r = lax.broadcasted_iota(jnp.int32, (rows, 1), 0)
            position = (r - (r & 7)) * 2 + b * 8 + (r & 7)
            valid = (position < valid_to).astype(F32)
            hidden = (before / (1.0 + jnp.exp(-before)) * valid).astype(BF)
            hid[:, :ffw] = hidden
            u_send[b] = adapter_scale * lax.dot_general(hidden, q_down, NT, preferred_element_type=F32)

        def down(h, s):
            n = ffw + ng * 16 if h is c else ffw
            parts = [
                jnp.dot(hid[:, :n], wp[1, 0:n, columns(h, s, f)], preferred_element_type=F32).reshape(chips, 8, sc)
                for f in range(2)
            ]
            return jnp.concatenate(parts, axis=1).astype(BF).reshape(nz, nx, 16, sc)

        rt, e1, e2 = {}, {}, {}

        def part(s, peer, lo, hi):
            return spart.at[s, peer, lo:hi] if s in sa else spart.at[s, lo:hi, peer]

        def peer_of(s, d):
            return zpeers[d] if s in sa else xpeers[d]

        def split(s):
            return 1 if s in sa else nx // 2

        def twin_part(s):
            tsend[s] = down(o, s)
            rt[s] = go(rcopy(tsend.at[s], trecv.at[s], rt_s.at[s], rt_r.at[s], twin))

        def own_part(s):
            mine = down(c, s).astype(F32)
            rt[s].wait_recv()
            spart[s] = (mine + trecv[s].astype(F32)).astype(BF)
            m = split(s)

            def put(i, ref, dst, d):
                e1[s, i] = go(rcopy(ref, dst, e1_s.at[s, i], e1_r.at[s, i], second_axis(s, d, sa)))

            if s not in RELAYED_SUM[layer]:
                put(2, part(s, peer_of(s, 1), 0, nx), r1.at[s, 0], 1)
                put(3, part(s, peer_of(s, 3), 0, nx), r1.at[s, 1], 3)
                put(4, part(s, peer_of(s, 2), 0, nx), far.at[s], 2)
                return
            put(0, part(s, peer_of(s, 2), 0, m), far.at[s, 0:m], 1)
            put(1, part(s, peer_of(s, 2), m, nx), far.at[s, m:nx], 3)
            put(2, part(s, peer_of(s, 1), m, nx), r1.at[s, 0, m:nx], 1)
            put(3, part(s, peer_of(s, 3), 0, m), r1.at[s, 1, 0:m], 3)

        def sum_part(s):
            m = split(s)
            for i, d, lo, hi in ((0, 1, 0, m), (1, 3, m, nx)):
                e1[s, i].wait_recv()
                far[s, lo:hi] = (far[s, lo:hi].astype(F32) + part(s, peer_of(s, d), lo, hi)[...].astype(F32)).astype(BF)
                e1[s, 4 + i] = go(rcopy(far.at[s, lo:hi], r1.at[s, i, lo:hi], e1_s.at[s, 4 + i], e1_r.at[s, 4 + i], second_axis(s, d, sa)))

        def down_block(b):
            u = go(rcopy(u_send.at[b], u_recv.at[b], low_s.at[1, b], low_r.at[1, b], twin))
            for s in BLOCKS[b]:
                twin_part(s)
            u.wait_recv()
            hid[:, ffw:] = (u_send[b] + u_recv[b]).astype(BF)
            if b == 0:
                arrived(py[1])
            for s in BLOCKS[b]:
                own_part(s)

        def sum_block(b):
            for s in BLOCKS[b]:
                if s in RELAYED_SUM[layer]:
                    sum_part(s)

        def scatter_second(b):
            for s in BLOCKS[b]:
                for i in range(2, 6 if s in RELAYED_SUM[layer] else 5):
                    e1[s, i].wait_recv()
                total = spart[s, zi].astype(F32) if s in sa else spart[s, :, xi].astype(F32)
                total = total + r1[s, 0].astype(F32) + r1[s, 1].astype(F32)
                if s not in RELAYED_SUM[layer]:
                    total = total + far[s].astype(F32)
                s1[s] = total.astype(BF)
                for d in (2, 1, 3):
                    peer = xpeers[d] if s in sa else zpeers[d]
                    e2[s, d] = go(rcopy(s1.at[s, peer], r2.at[s, d - 1], e2_s.at[s, d - 1], e2_r.at[s, d - 1], first_axis(s, d, sa)))

        relay = []

        def finish(b):
            for s in BLOCKS[b]:
                k = s % 2
                total = s1[s, xi if s in sa else zi].astype(F32)
                for d in NEAR_FIRST:
                    e2[s, d].wait_recv()
                    total = total + r2[s, d - 1].astype(F32)
                total = total + xg[c, s, zi, xi].astype(F32)
                fb[s] = total.astype(BF)
                fs[b, :, k * kc:k * kc + sc] = total[:8]
                fs[b, :, k * kc + sc:(k + 1) * kc] = total[8:]
                if layer:
                    continue
                here = [
                    rcopy(fb.at[s], at_first(s, 0), rel_s.at[s, d], g1_r.at[s, d], {"section": 1, **first_axis(s, d, GATHER_A[1])})
                    for d in range(nx)
                ]
                relay.extend(here)
                start(here)

        up_block(0)
        if layer == 1:
            gather_second(1)
        down_block(0)
        up_block(1)
        sum_block(0)
        down_block(1)
        scatter_second(0)
        sum_block(1)
        finish(0)
        scatter_second(1)
        finish(1)

        fin = go(rcopy(fs.at[o], fr, bar_s.at[2], bar_r.at[2], twin))
        out_ref[0, :, mine_at] = fs[c].astype(BF)
        fin.wait_recv()
        out_ref[0, :, other_at] = fr[...].astype(BF)
        if layer == 0:
            sends.append(xtw)
            sends.extend(g1[s, d] for s in range(STREAMS) for d in range(1, nx))
        @pl.when(is_source)
        def _():
            for k in pz:
                k.wait_send()

        for k in sends + relay:
            k.wait_send()

    @pl.when(sec0)
    def _():
        run(0)

    @pl.when(sec1)
    def _():
        run(1)


def body(inputs, lengths, norm_gain, base_weight, factor_p, factor_q):
    ng = lax.axis_size("group")
    nx = NX
    nz = lax.axis_size("tp") // 2 // nx
    assert nx == nz
    d_model = inputs.shape[1]
    ffw = base_weight.shape[3]
    rows = nz * nx * 8
    hc, pc = d_model // 2, d_model // (nz * nx)
    sc = hc // STREAMS
    vmem = pl.BlockSpec(memory_space=pltpu.VMEM)
    dma = pltpu.SemaphoreType.DMA
    n3 = max(nx, ng) - 1
    return pl.pallas_call(
        functools.partial(kernel, nz, nx, ng),
        out_shape=jax.ShapeDtypeStruct((1, 8, d_model), BF),
        in_specs=[
            vmem,
            pl.BlockSpec(memory_space=pltpu.SMEM),
            vmem,
            pl.BlockSpec(memory_space=pl.ANY),
            vmem,
            vmem,
        ],
        out_specs=vmem,
        scratch_shapes=[
            pltpu.VMEM((8, hc), F32),
            pltpu.VMEM((8, hc), F32),
            pltpu.VMEM((2, STREAMS, nz, nx, 16, sc), BF),
            pltpu.VMEM((2, ffw + ng * 16, d_model), BF),
            pltpu.VMEM((2, 16, pc), BF),
            pltpu.VMEM((2, 16, pc), BF),
            pltpu.VMEM((2, ng, 16, ffw), BF),
            pltpu.VMEM((rows, ffw + ng * 16), F32),
            pltpu.VMEM((rows, ffw + ng * 16), BF),
            pltpu.VMEM((STREAMS, nz, nx, 16, sc), BF),
            pltpu.VMEM((STREAMS, nz, nx, 16, sc), BF),
            pltpu.VMEM((STREAMS, nz, nx, 16, sc), BF),
            pltpu.VMEM((STREAMS, nx, 16, sc), BF),
            pltpu.VMEM((STREAMS, 2, nx, 16, sc), BF),
            pltpu.VMEM((STREAMS, nx, 16, sc), BF),
            pltpu.VMEM((STREAMS, nx - 1, 16, sc), BF),
            pltpu.VMEM((STREAMS, 16, sc), BF),
            pltpu.VMEM((2, 8, hc), F32),
            pltpu.VMEM((8, hc), F32),
            pltpu.VMEM((2, rows, ng * 16), F32),
            pltpu.VMEM((2, rows, ng * 16), F32),
            pltpu.VMEM((2, rows, ng * 16), F32),
            pltpu.VMEM((2, rows, ng * 16), F32),
            dma((2,)),
            dma((3,)), dma((3,)),
            dma((STREAMS, nx)), dma((STREAMS, nx)),
            dma((STREAMS, nx, nx)), dma((STREAMS, nx, nx)),
            dma((STREAMS, nx)), dma((STREAMS, nx)),
            dma((STREAMS, nx)), dma((STREAMS, nx)),
            dma((n3,)), dma((n3,)),
            dma((n3, nz // 2)), dma((n3, nz // 2)),
            dma((2, n3)), dma((2, n3)),
            dma((2, 2)), dma((2, 2)),
            dma((n3,)), dma((n3,)),
            dma((STREAMS,)), dma((STREAMS,)),
            dma((STREAMS, 6)), dma((STREAMS, 6)),
            dma((STREAMS, nx)), dma((STREAMS, nx)),
            dma((STREAMS, nx)),
        ],
        compiler_params=pltpu.CompilerParams(
            collective_id=0, has_side_effects=True, vmem_limit_bytes=56 * 1024 * 1024
        ),
    )(inputs, lengths, norm_gain, jnp.swapaxes(base_weight[0], 1, 2), factor_p[0], factor_q[0])


def solution(mesh):
    return jax.shard_map(
        body,
        mesh=mesh,
        in_specs=(
            P(("group", "tp"), None),
            P("group"),
            P("section", None),
            P("section", None, None, "tp"),
            P("section", None, "group", "tp"),
            P("section", None, "group", "tp"),
        ),
        out_specs=P("section", ("group", "tp"), None),
        check_vma=False,
    )
```
